512 devices in a mesh: dp: 64 (over x, z, core), tensor: 8 (over y).
Axes of the slice: x: 4, y: 8, z: 8, core: 2. Of those that a mesh axis runs over, the one named last changes fastest.
Arguments:
- grads: float32 [64, 4096, 512], P('dp', 'tensor'), may hold values from -80 to 80
- signs: int32 [4096, 512], P('tensor'), may hold values from -1 to 1, as said below
- dither: int32 [64, 4096, 512], P('dp', 'tensor'), may hold values from 0 to 4095
Outputs:
- mean_grad: float32 [4096, 512], P('tensor')
- quant_step: float32 [], replicated
The draws below stay inside these ranges and needn't reach their ends.
Inputs may be any that keep to these rules, and one draw needn't show every extreme that they name: `signs`: every entry is -1 or 1.
All inputs are finite; a program needn't handle non-finite values. Where the reference program divides by a largest or mean magnitude, that divisor is 1e-20 or more.
Results may differ from the reference program's by a relative error of at most 0.0008.
Values sent between devices are 32-bit elements; how exact they have to be, the bound alone decides.
No kernel may reach another device: no remote copies, remote signals or barrier semaphores. Data moves between devices by JAX's collectives and lax.ppermute only.
A program may use at most 64 MiB of HBM per device.

```python
import math
import jax
import jax.numpy as jnp
from jax import lax

BLOCK = 512
BLOCKS = 512
ROWS = 4096
N_DP = 64
N_TENSOR = 8


def draw_grads(key, part):
    key = jax.random.fold_in(key, 11)
    first, second = jax.random.split(key, 2)
    shape = (N_DP, N_TENSOR * BLOCKS, BLOCK)
    rise = 1.0 + 2.0 * jnp.arange(N_DP, dtype=jnp.float32)[:, None, None] / max(N_DP - 1, 1)
    block_scale = jnp.exp(jax.random.uniform(second, (1, N_TENSOR * BLOCKS, 1), jnp.float32, jnp.log(0.3), jnp.log(3.0)))
    values = jnp.clip(jax.random.normal(first, shape, jnp.float32), -6.0, 6.0)
    return values * rise * block_scale


def draw_signs(key, part):
    key = jax.random.fold_in(key, 23)
    flips = jax.random.randint(key, (N_TENSOR * BLOCKS, BLOCK), 0, 2)
    return (2 * flips - 1).astype(jnp.int32)


def place_ends(result, stream_key, least, largest):
    dims = result.shape
    place = [jax.random.randint(jax.random.fold_in(stream_key, axis), (), 0, dims[axis]) for axis in range(len(dims))]
    result = result.at[tuple(place)].set(least)
    longest = dims.index(max(dims))
    place[longest] = (place[longest] + 1) % dims[longest]
    return result.at[tuple(place)].set(largest)


def setup_inputs(seed: int = 0) -> dict:
    seeds = jax.random.split(jax.random.key(seed), 4)
    grads = draw_grads(jax.random.fold_in(seeds[3], 71), 0)
    signs = draw_signs(jax.random.fold_in(seeds[3], 71), 0)
    dither = place_ends(jax.random.randint(seeds[2], (N_DP, ROWS, BLOCK), 0, 4096), jax.random.fold_in(seeds[2], 1), 0, 4095).astype(jnp.int32)
    return dict(grads=grads, signs=signs, dither=dither)


def hadamard(length):
    indices = jnp.arange(length, dtype=jnp.int32)
    common_bits = jnp.bitwise_and(indices[:, None], indices[None, :])
    parity = jnp.zeros((length, length), jnp.int32)
    for position in range(length.bit_length()):
        parity = parity + jnp.bitwise_and(jnp.right_shift(common_bits, position), 1)
    return (1 - 2 * (parity % 2)).astype(jnp.float32) / math.sqrt(length)

def reference(grads, signs, dither):
    matrix = hadamard(BLOCK)
    sign_vals = signs.astype(jnp.float32)
    signed = grads * sign_vals[None]
    rotated = jnp.dot(signed.reshape(-1, BLOCK), matrix, precision=lax.Precision.HIGHEST, preferred_element_type=jnp.float32).reshape(signed.shape)
    peak = jnp.max(jnp.abs(rotated))
    scale = 127.0 / peak
    codes = jnp.floor(rotated * scale + dither.astype(jnp.float32) * 2.0 ** (-12))
    total = lax.optimization_barrier(jnp.sum(codes, axis=0))
    quant_step = peak / 127.0
    back = jnp.dot(total, matrix, precision=lax.Precision.HIGHEST, preferred_element_type=jnp.float32)
    mean_grad = sign_vals * (back * (quant_step / N_DP))
    return (mean_grad, quant_step)
```

```python
import math

import jax
import jax.numpy as jnp
import numpy as np
from jax import lax
from jax.experimental import pallas as pl
from jax.experimental.pallas import tpu as pltpu
from jax.sharding import Mesh, PartitionSpec as P

Z, CORES = 8, 2
CHIPS = ("x", "z")
STRIPE = 128


def signs_matrix(length):
    matrix = np.ones((1, 1), np.float32)
    while matrix.shape[0] < length:
        matrix = np.block([[matrix, matrix], [matrix, -matrix]])
    return jnp.asarray(matrix, jnp.bfloat16)


def butterfly(values):
    half = values.shape[1] // 2
    left, right = values[:, :half], values[:, half:]
    return jnp.concatenate([left + right, left - right], axis=0)


def parts_of(values, count):
    parts = []
    for _ in range(count):
        part = values.astype(jnp.bfloat16)
        parts.append(part)
        values = values - part.astype(jnp.float32)
    return parts


def transform(values, matrix, count):
    rows, length = values.shape
    parts = parts_of(butterfly(values), count)
    out = jnp.dot(parts[-1], matrix, preferred_element_type=jnp.float32)
    for part in parts[-2::-1]:
        out = out + jnp.dot(part, matrix, preferred_element_type=jnp.float32)
    out = out * (1.0 / math.sqrt(length))
    return jnp.concatenate([out[:rows], out[rows:]], axis=1)


def rotate_kernel(place, grads, signs, dither, matrix, own, send, top):
    step = pl.program_id(0)
    steps = pl.num_programs(0) // 2
    half = own.shape[0]
    rotated = transform(grads[...] * signs[...].astype(jnp.float32), matrix[...], 3)
    highest = jnp.max(jnp.abs(rotated).reshape(STRIPE // 8, 8, -1), axis=0)

    @pl.when(step == 0)
    def _():
        top[...] = highest

    @pl.when(step > 0)
    def _():
        top[...] = jnp.maximum(top[...], highest)

    @pl.when(step < steps)
    def _():
        at = pl.multiple_of(step * STRIPE, STRIPE)
        send[pl.ds(at, STRIPE), :] = rotated
        send[pl.ds(pl.multiple_of(half + at, STRIPE), STRIPE), :] = dither[...].astype(jnp.float32)

    @pl.when(step >= steps)
    def _():
        own[pl.ds(pl.multiple_of((step - steps) * STRIPE, STRIPE), STRIPE), :] = rotated

    @pl.when(step == 2 * steps - 1)
    def _():
        send[2 * half :, :] = top[...]


def rotate(place, grads, signs, dither, matrix):
    rows, length = grads.shape
    half = rows // 2
    steps = half // STRIPE

    def block(i, place):
        core = jnp.where(i < steps, 1 - place[0], place[0])
        return (core * steps + lax.rem(i, steps), 0)

    def others(i, place):
        return ((1 - place[0]) * steps + jnp.minimum(i, steps - 1), 0)

    whole = lambda i, place: (0, 0)
    return pl.pallas_call(
        rotate_kernel,
        grid_spec=pltpu.PrefetchScalarGridSpec(
            num_scalar_prefetch=1,
            grid=(2 * steps,),
            in_specs=[
                pl.BlockSpec((STRIPE, length), block),
                pl.BlockSpec((STRIPE, length), block),
                pl.BlockSpec((STRIPE, length), others),
                pl.BlockSpec(matrix.shape, whole),
            ],
            out_specs=[
                pl.BlockSpec((half, length), whole),
                pl.BlockSpec((rows + 8, length), whole),
            ],
            scratch_shapes=[pltpu.VMEM((8, length), jnp.float32)],
        ),
        out_shape=[
            jax.ShapeDtypeStruct((half, length), jnp.float32),
            jax.ShapeDtypeStruct((rows + 8, length), jnp.float32),
        ],
        compiler_params=pltpu.CompilerParams(vmem_limit_bytes=24 * 2**20),
        name="rotate",
    )(place, grads, signs, dither, matrix)


def chip_top_kernel(mine, theirs, out):
    out[...] = jnp.full(out.shape, jnp.max(jnp.maximum(mine[...], theirs[...])), jnp.float32)


def chip_top(sent, received, peers):
    rows, length = sent.shape
    last = pl.BlockSpec((8, length), lambda i: (rows // 8 - 1, 0))
    return pl.pallas_call(
        chip_top_kernel,
        grid=(1,),
        in_specs=[last, last],
        out_specs=pl.BlockSpec((peers, 128), lambda i: (0, 0)),
        out_shape=jax.ShapeDtypeStruct((peers, 128), jnp.float32),
        name="chip_top",
    )(sent, received)


def codes_kernel(place, tops, own, dither, other, other_dither, codes, quant_step):
    top = jnp.max(tops[...], axis=0, keepdims=True)
    scale = jnp.concatenate([127.0 / top] * (own.shape[1] // 128), axis=1)
    first = jnp.floor(own[...] * scale + dither[...].astype(jnp.float32) * 2.0 ** (-12))
    second = jnp.floor(other[...] * scale + other_dither[...] * 2.0 ** (-12))
    codes[...] = first + second
    quant_step[0, 0] = jnp.max(top / 127.0)


def chip_codes(place, tops, own, dither, received):
    half, length = own.shape
    steps = half // STRIPE
    stripe = lambda index: pl.BlockSpec((STRIPE, length), index)
    return pl.pallas_call(
        codes_kernel,
        grid_spec=pltpu.PrefetchScalarGridSpec(
            num_scalar_prefetch=1,
            grid=(steps,),
            in_specs=[
                pl.BlockSpec(tops.shape, lambda i, place: (0, 0)),
                stripe(lambda i, place: (i, 0)),
                stripe(lambda i, place: (place[0] * steps + i, 0)),
                stripe(lambda i, place: (i, 0)),
                stripe(lambda i, place: (steps + i, 0)),
            ],
            out_specs=[
                stripe(lambda i, place: (i, 0)),
                pl.BlockSpec(memory_space=pltpu.SMEM),
            ],
        ),
        out_shape=[
            jax.ShapeDtypeStruct((half, length), jnp.float32),
            jax.ShapeDtypeStruct((1, 1), jnp.float32),
        ],
        compiler_params=pltpu.CompilerParams(vmem_limit_bytes=24 * 2**20),
        name="chip_codes",
    )(place, tops, own, dither, received, received)


def mean_kernel(replicas, place, codes, signs, matrix, quant_step, out):
    total = jnp.sum(codes[...], axis=0)
    back = transform(total, matrix[...], 2)
    mean = signs[...].astype(jnp.float32) * (back * (quant_step[0, 0] * (1.0 / replicas)))
    out[...] = jnp.broadcast_to(mean[None], out.shape)


def owned_mean(replicas, place, codes, signs, matrix, quant_step):
    peers, rows, length = codes.shape
    whole = lambda i, place: (0, 0, 0)
    return pl.pallas_call(
        lambda *refs: mean_kernel(replicas, *refs),
        grid_spec=pltpu.PrefetchScalarGridSpec(
            num_scalar_prefetch=1,
            grid=(1,),
            in_specs=[
                pl.BlockSpec(codes.shape, whole),
                pl.BlockSpec((rows, length), lambda i, place: (place[1], 0)),
                pl.BlockSpec(matrix.shape, lambda i, place: (0, 0)),
                pl.BlockSpec(memory_space=pltpu.SMEM),
            ],
            out_specs=pl.BlockSpec(codes.shape, whole),
        ),
        out_shape=jax.ShapeDtypeStruct(codes.shape, jnp.float32),
        name="owned_mean",
    )(place, codes, signs, matrix, quant_step)


def shards(grads, signs, dither):
    _, rows, length = grads.shape
    chips = lax.axis_size(CHIPS)
    peers = lax.axis_size(CHIPS + ("tensor",))
    core = lax.axis_index("core")
    place = jnp.stack([core, core * chips + lax.axis_index(CHIPS)]).astype(jnp.int32)
    swap = [(0, 1), (1, 0)]
    matrix = signs_matrix(length // 2)

    own, send = rotate(place, grads[0], signs, dither[0], matrix)
    received = lax.ppermute(send, "core", swap)

    tops = chip_top(send, received, peers).reshape(peers, 1, 128)
    tops = lax.all_to_all(tops, CHIPS + ("tensor",), 0, 0).reshape(peers, 128)

    codes, quant_step = chip_codes(place, tops, own, dither[0], received)
    codes = codes.reshape(chips, rows // 2 // chips, length)
    codes = lax.all_to_all(codes, CHIPS, 0, 0)

    mean = owned_mean(CORES * chips, place, codes, signs, matrix, quant_step)
    mean = lax.all_to_all(mean, CHIPS, 0, 0).reshape(rows // 2, length)

    other = lax.ppermute(mean, "core", swap)
    low = core == 0
    mean_grad = jnp.concatenate([jnp.where(low, mean, other), jnp.where(low, other, mean)], axis=0)
    return (mean_grad, quant_step.reshape(()))


def solution(mesh):
    tensor = mesh.shape["tensor"]
    devices = mesh.devices.reshape(-1, Z, CORES, tensor)
    fine = Mesh(devices, ("x", "z", "core", "tensor"))
    dp = ("x", "z", "core")
    return jax.shard_map(
        shards,
        mesh=fine,
        in_specs=(P(dp, "tensor", None), P("tensor", None), P(dp, "tensor", None)),
        out_specs=(P("tensor", None), P()),
        check_vma=False,
    )
```

```python
import math

import jax
import jax.numpy as jnp
import numpy as np
from jax import lax
from jax.experimental import pallas as pl
from jax.experimental.pallas import tpu as pltpu
from jax.sharding import Mesh, PartitionSpec as P

Z, CORES = 8, 2
CHIPS = ("x", "z")
STRIPE = 128


def signs_matrix(length):
    matrix = np.ones((1, 1), np.float32)
    while matrix.shape[0] < length:
        matrix = np.block([[matrix, matrix], [matrix, -matrix]])
    return jnp.asarray(matrix, jnp.bfloat16)


def butterfly(values):
    half = values.shape[1] // 2
    left, right = values[:, :half], values[:, half:]
    return jnp.concatenate([left + right, left - right], axis=0)


def parts_of(values, count):
    parts = []
    for _ in range(count):
        part = values.astype(jnp.bfloat16)
        parts.append(part)
        values = values - part.astype(jnp.float32)
    return parts


def transform(values, matrix, count):
    rows, length = values.shape
    parts = parts_of(butterfly(values), count)
    out = jnp.dot(parts[-1], matrix, preferred_element_type=jnp.float32)
    for part in parts[-2::-1]:
        out = out + jnp.dot(part, matrix, preferred_element_type=jnp.float32)
    out = out * (1.0 / math.sqrt(length))
    return jnp.concatenate([out[:rows], out[rows:]], axis=1)


def rotate_kernel(
    place, grads, signs, dither, matrix_in, own, own_dither, send, matrix, own_signs,
    grads_buf, signs_buf, dither_buf, fetched, kept,
):
    rows, length = grads.shape
    half = rows // 2
    steps = half // STRIPE
    mine = place[0] * half
    others = half - mine
    starts = [others + i * STRIPE for i in range(steps)] + [mine + i * STRIPE for i in range(steps)]

    def fetch(i, which):
        at = pl.multiple_of(starts[i], STRIPE)
        source, target = ((grads, grads_buf), (signs, signs_buf), (dither, dither_buf))[which]
        return pltpu.make_async_copy(
            source.at[pl.ds(at, STRIPE), :], target.at[pl.ds(i * STRIPE, STRIPE), :], fetched.at[which, i]
        )

    copies = [[fetch(i, which) for which in range(3 if i < steps else 2)] for i in range(2 * steps)]
    get_matrix = pltpu.make_async_copy(matrix_in, matrix, kept.at[0])
    get_dither = pltpu.make_async_copy(
        dither.at[pl.ds(pl.multiple_of(mine, STRIPE), half), :], own_dither, kept.at[1]
    )
    for i, group in enumerate(copies):
        group[0].start()
        group[1].start()
        if i == 0:
            get_matrix.start()
    for group in copies[:steps]:
        group[2].start()
    get_dither.start()
    get_matrix.wait()

    top = None
    for i, group in enumerate(copies):
        here = pl.ds(i * STRIPE, STRIPE)
        group[0].wait()
        group[1].wait()
        rotated = transform(grads_buf[here, :] * signs_buf[here, :].astype(jnp.float32), matrix[...], 3)
        highest = jnp.max(jnp.abs(rotated).reshape(STRIPE // 8, 8, length), axis=0)
        top = highest if top is None else jnp.maximum(top, highest)
        if i < steps:
            send[here, :] = rotated
        else:
            own[pl.ds((i - steps) * STRIPE, STRIPE), :] = rotated
    send[rows:, :] = top
    for i, group in enumerate(copies[:steps]):
        group[2].wait()
        here = pl.ds(i * STRIPE, STRIPE)
        send[pl.ds(half + i * STRIPE, STRIPE), :] = dither_buf[here, :].astype(jnp.float32)
    mean_rows = own_signs.shape[0]
    at = pl.multiple_of(half + place[1] * mean_rows, mean_rows)
    own_signs[...] = signs_buf[pl.ds(at, mean_rows), :].astype(jnp.float32)
    get_dither.wait()


VMEM = pl.BlockSpec(memory_space=pltpu.VMEM)
SMEM = pl.BlockSpec(memory_space=pltpu.SMEM)
HBM = pl.BlockSpec(memory_space=pltpu.HBM)
LIMIT = pltpu.CompilerParams(vmem_limit_bytes=16 * 2**20)


def rotate(place, grads, signs, dither, matrix, mean_rows):
    rows, length = grads.shape
    half = rows // 2
    steps = half // STRIPE
    return pl.pallas_call(
        rotate_kernel,
        in_specs=[SMEM, HBM, HBM, HBM, HBM],
        out_specs=[VMEM] * 5,
        out_shape=[
            jax.ShapeDtypeStruct((half, length), jnp.float32),
            jax.ShapeDtypeStruct((half, length), jnp.int32),
            jax.ShapeDtypeStruct((rows + 8, length), jnp.float32),
            jax.ShapeDtypeStruct(matrix.shape, matrix.dtype),
            jax.ShapeDtypeStruct((mean_rows, length), jnp.float32),
        ],
        scratch_shapes=[
            pltpu.VMEM((rows, length), jnp.float32),
            pltpu.VMEM((rows, length), jnp.int32),
            pltpu.VMEM((half, length), jnp.int32),
            pltpu.SemaphoreType.DMA((3, 2 * steps)),
            pltpu.SemaphoreType.DMA((2,)),
        ],
        compiler_params=LIMIT,
        name="rotate",
    )(place, *(pltpu.with_memory_space_constraint(a, pltpu.HBM) for a in (grads, signs, dither, matrix)))


def chip_top_kernel(sent, received, out):
    last = pl.ds(sent.shape[0] - 8, 8)
    top = jnp.max(jnp.maximum(sent[last, :], received[last, :]))
    out[...] = jnp.full(out.shape, top, jnp.float32)


def chip_top(sent, received, peers):
    return pl.pallas_call(
        chip_top_kernel,
        in_specs=[VMEM, VMEM],
        out_specs=VMEM,
        out_shape=jax.ShapeDtypeStruct((peers, 128), jnp.float32),
        compiler_params=LIMIT,
        name="chip_top",
    )(sent, received)


def codes_kernel(tops, own, dither, received, codes, quant_step):
    half, length = own.shape
    top = jnp.max(tops[...], axis=0, keepdims=True)
    scale = jnp.concatenate([127.0 / top] * (length // 128), axis=1)
    for i in range(0, half, STRIPE):
        here, there = pl.ds(i, STRIPE), pl.ds(half + i, STRIPE)
        first = jnp.floor(own[here, :] * scale + dither[here, :].astype(jnp.float32) * 2.0 ** (-12))
        second = jnp.floor(received[here, :] * scale + received[there, :] * 2.0 ** (-12))
        codes[here, :] = first + second
    quant_step[0, 0] = jnp.max(top / 127.0)


def chip_codes(tops, own, dither, received):
    return pl.pallas_call(
        codes_kernel,
        in_specs=[VMEM] * 4,
        out_specs=[VMEM, SMEM],
        out_shape=[
            jax.ShapeDtypeStruct(own.shape, jnp.float32),
            jax.ShapeDtypeStruct((1, 1), jnp.float32),
        ],
        compiler_params=LIMIT,
        name="chip_codes",
    )(tops, own, dither, received)


def mean_kernel(replicas, codes, signs, matrix, quant_step, out):
    total = jnp.sum(codes[...], axis=0)
    back = transform(total, matrix[...], 2)
    mean = signs[...] * (back * (quant_step[0, 0] * (1.0 / replicas)))
    out[...] = jnp.broadcast_to(mean[None], out.shape)


def owned_mean(replicas, codes, signs, matrix, quant_step):
    return pl.pallas_call(
        lambda *refs: mean_kernel(replicas, *refs),
        in_specs=[VMEM, VMEM, VMEM, SMEM],
        out_specs=VMEM,
        out_shape=jax.ShapeDtypeStruct(codes.shape, jnp.float32),
        compiler_params=LIMIT,
        name="owned_mean",
    )(codes, signs, matrix, quant_step)


PIECES = 4


def store_half(place, half, out, done, which):
    rows = half.shape[0]
    core = place[0] if which == 0 else 1 - place[0]
    piece = rows // PIECES
    copies = [
        pltpu.make_async_copy(
            half.at[pl.ds(i * piece, piece), :],
            out.at[pl.ds(pl.multiple_of(core * rows + i * piece, piece), piece), :],
            done.at[i],
        )
        for i in range(PIECES)
    ]
    for copy in copies:
        copy.start()
    for copy in copies:
        copy.wait()


def store_mine_kernel(place, half, out, done):
    store_half(place, half, out, done, 0)


def store_other_kernel(place, half, _, out, done):
    store_half(place, half, out, done, 1)


def store_mine(place, half):
    rows, length = half.shape
    return pl.pallas_call(
        store_mine_kernel,
        in_specs=[SMEM, VMEM],
        out_specs=HBM,
        out_shape=jax.ShapeDtypeStruct((2 * rows, length), half.dtype),
        scratch_shapes=[pltpu.SemaphoreType.DMA((PIECES,))],
        compiler_params=LIMIT,
        name="store_mine",
    )(place, half)


def store_other(place, half, out):
    return pl.pallas_call(
        store_other_kernel,
        in_specs=[SMEM, VMEM, HBM],
        out_specs=HBM,
        out_shape=jax.ShapeDtypeStruct(out.shape, out.dtype),
        scratch_shapes=[pltpu.SemaphoreType.DMA((PIECES,))],
        input_output_aliases={2: 0},
        compiler_params=LIMIT,
        name="store_other",
    )(place, half, out)


def shards(grads, signs, dither):
    _, rows, length = grads.shape
    chips = lax.axis_size(CHIPS)
    peers = lax.axis_size(CHIPS + ("tensor",))
    core = lax.axis_index("core")
    place = jnp.stack([core, lax.axis_index(CHIPS)]).astype(jnp.int32)
    swap = [(0, 1), (1, 0)]
    matrix = signs_matrix(length // 2)
    mean_rows = rows // 2 // chips

    own, own_dither, send, matrix, own_signs = rotate(place, grads[0], signs, dither[0], matrix, mean_rows)
    received = lax.ppermute(send, "core", swap)

    tops = chip_top(send, received, peers).reshape(peers, 1, 128)
    tops = lax.all_to_all(tops, CHIPS + ("tensor",), 0, 0).reshape(peers, 128)

    codes, quant_step = chip_codes(tops, own, own_dither, received)
    codes = lax.all_to_all(codes.reshape(chips, mean_rows, length), CHIPS, 0, 0)

    mean = owned_mean(CORES * chips, codes, own_signs, matrix, quant_step)
    mean = lax.all_to_all(mean, CHIPS, 0, 0).reshape(rows // 2, length)

    other = lax.ppermute(mean, "core", swap)
    mean_grad = store_other(place, other, store_mine(place, mean))
    return (mean_grad, quant_step.reshape(()))


def solution(mesh):
    tensor = mesh.shape["tensor"]
    devices = mesh.devices.reshape(-1, Z, CORES, tensor)
    fine = Mesh(devices, ("x", "z", "core", "tensor"))
    dp = ("x", "z", "core")
    return jax.shard_map(
        shards,
        mesh=fine,
        in_specs=(P(dp, "tensor", None), P("tensor", None), P(dp, "tensor", None)),
        out_specs=(P("tensor", None), P()),
        check_vma=False,
    )
```

```python
import math

import jax
import jax.numpy as jnp
import numpy as np
from jax import lax
from jax.experimental import pallas as pl
from jax.experimental.pallas import tpu as pltpu
from jax.sharding import Mesh, PartitionSpec as P

Z, CORES = 8, 2
CHIPS = ("x", "z")
NEAR, FAR = ("core", "tensor"), ("x", "z")
STRIPE = 64


def signs_matrix(length):
    matrix = np.ones((1, 1), np.float32)
    while matrix.shape[0] < length:
        matrix = np.block([[matrix, matrix], [matrix, -matrix]])
    return jnp.asarray(matrix, jnp.bfloat16)


def butterfly(values):
    half = values.shape[1] // 2
    left, right = values[:, :half], values[:, half:]
    return jnp.concatenate([left + right, left - right], axis=0)


def parts_of(values, count):
    parts = []
    for _ in range(count):
        part = values.astype(jnp.bfloat16)
        parts.append(part)
        values = values - part.astype(jnp.float32)
    return parts


def transform(values, matrix, count):
    rows, length = values.shape
    parts = jnp.concatenate(parts_of(butterfly(values), count), axis=0)
    products = jnp.dot(parts, matrix, preferred_element_type=jnp.float32)
    out = products[-2 * rows :]
    for i in range(count - 2, -1, -1):
        out = out + products[2 * rows * i : 2 * rows * (i + 1)]
    out = out * (1.0 / math.sqrt(length))
    return jnp.concatenate([out[:rows], out[rows:]], axis=1)


def rotate_kernel(
    grads, signs, dither, matrix_in, own, own_dither, send, tops, matrix, own_signs,
    grads_buf, signs_buf, dither_buf, fetched, kept,
):
    rows, length = grads.shape
    half = rows // 2
    mine = lax.axis_index("core") * half
    others = half - mine
    low, high = pl.ds(0, half), pl.ds(half, half)

    def at(start):
        return pl.ds(pl.multiple_of(start, half), half)

    def fetch(source, start, target, place, semaphore):
        return pltpu.make_async_copy(source.at[at(start), :], target.at[place, :], semaphore)

    stages = [
        (place, fetch(grads, start, grads_buf, place, fetched.at[0, i]), fetch(signs, start, signs_buf, place, fetched.at[1, i]))
        for i, (place, start) in enumerate(((low, others), (high, mine)))
    ]
    get_matrix = pltpu.make_async_copy(matrix_in, matrix, kept.at[0])
    get_others = pltpu.make_async_copy(dither.at[at(others), :], dither_buf, kept.at[1])
    get_mine = pltpu.make_async_copy(dither.at[at(mine), :], own_dither, kept.at[2])
    get_matrix.start()
    for _, get_grads, get_signs in stages:
        get_grads.start()
        get_signs.start()
    get_others.start()
    get_mine.start()
    get_matrix.wait()

    top = jnp.zeros((8, length), jnp.float32)
    for (place, get_grads, get_signs), result in zip(stages, (send, own)):
        get_grads.wait()
        get_signs.wait()
        rotated = transform(grads_buf[place, :] * signs_buf[place, :].astype(jnp.float32), matrix[...], 3)
        top = jnp.maximum(top, jnp.max(jnp.abs(rotated).reshape(half // 8, 8, length), axis=0))
        result[low, :] = rotated
    tops[...] = jnp.full(tops.shape, jnp.max(top), jnp.float32)
    get_others.wait()
    send[high, :] = dither_buf[...].astype(jnp.float32)
    mean_rows = own_signs.shape[0]
    chip = lax.axis_index("x") * lax.axis_size("z") + lax.axis_index("z")
    here = pl.ds(pl.multiple_of(half + chip * mean_rows, mean_rows), mean_rows)
    own_signs[...] = signs_buf[here, :].astype(jnp.float32)
    get_mine.wait()


VMEM = pl.BlockSpec(memory_space=pltpu.VMEM)
SMEM = pl.BlockSpec(memory_space=pltpu.SMEM)
HBM = pl.BlockSpec(memory_space=pltpu.HBM)
LIMIT = pltpu.CompilerParams(vmem_limit_bytes=16 * 2**20)


def rotate(grads, signs, dither, matrix, mean_rows, peers):
    rows, length = grads.shape
    half = rows // 2
    return pl.pallas_call(
        rotate_kernel,
        in_specs=[HBM] * 4,
        out_specs=[VMEM] * 6,
        out_shape=[
            jax.ShapeDtypeStruct((half, length), jnp.float32),
            jax.ShapeDtypeStruct((half, length), jnp.int32),
            jax.ShapeDtypeStruct((rows, length), jnp.float32),
            jax.ShapeDtypeStruct((peers, 128), jnp.float32),
            jax.ShapeDtypeStruct(matrix.shape, matrix.dtype),
            jax.ShapeDtypeStruct((mean_rows, length), jnp.float32),
        ],
        scratch_shapes=[
            pltpu.VMEM((rows, length), jnp.float32),
            pltpu.VMEM((rows, length), jnp.int32),
            pltpu.VMEM((half, length), jnp.int32),
            pltpu.SemaphoreType.DMA((2, 2)),
            pltpu.SemaphoreType.DMA((3,)),
        ],
        compiler_params=LIMIT,
        name="rotate",
    )(*(pltpu.with_memory_space_constraint(a, pltpu.HBM) for a in (grads, signs, dither, matrix)))


def highest_kernel(tops, out):
    out[...] = jnp.broadcast_to(jnp.max(tops[...], axis=0, keepdims=True), out.shape)


def highest(tops, peers):
    return pl.pallas_call(
        highest_kernel,
        in_specs=[VMEM],
        out_specs=VMEM,
        out_shape=jax.ShapeDtypeStruct((peers, 128), jnp.float32),
        compiler_params=LIMIT,
        name="highest",
    )(tops)


def exchange(tops, axes):
    peers, lanes = tops.shape
    return lax.all_to_all(tops.reshape(peers, 1, lanes), axes, 0, 0).reshape(peers, lanes)


def codes_kernel(tops, own, dither, received, codes, quant_step):
    half, length = own.shape
    top = jnp.max(tops[...], axis=0, keepdims=True)
    scale = jnp.concatenate([127.0 / top] * (length // 128), axis=1)
    for i in range(0, half, STRIPE):
        here, there = pl.ds(i, STRIPE), pl.ds(half + i, STRIPE)
        first = jnp.floor(own[here, :] * scale + dither[here, :].astype(jnp.float32) * 2.0 ** (-12))
        second = jnp.floor(received[here, :] * scale + received[there, :] * 2.0 ** (-12))
        codes[here, :] = first + second
    quant_step[0, 0] = jnp.max(top / 127.0)


def chip_codes(tops, own, dither, received):
    return pl.pallas_call(
        codes_kernel,
        in_specs=[VMEM] * 4,
        out_specs=[VMEM, SMEM],
        out_shape=[
            jax.ShapeDtypeStruct(own.shape, jnp.float32),
            jax.ShapeDtypeStruct((1, 1), jnp.float32),
        ],
        compiler_params=LIMIT,
        name="chip_codes",
    )(tops, own, dither, received)


def mean_kernel(replicas, codes, signs, matrix, quant_step, out):
    total = jnp.sum(codes[...], axis=0)
    back = transform(total, matrix[...], 2)
    mean = signs[...] * (back * (quant_step[0, 0] * (1.0 / replicas)))
    out[...] = jnp.broadcast_to(mean[None], out.shape)


def owned_mean(replicas, codes, signs, matrix, quant_step):
    return pl.pallas_call(
        lambda *refs: mean_kernel(replicas, *refs),
        in_specs=[VMEM, VMEM, VMEM, SMEM],
        out_specs=VMEM,
        out_shape=jax.ShapeDtypeStruct(codes.shape, jnp.float32),
        compiler_params=LIMIT,
        name="owned_mean",
    )(codes, signs, matrix, quant_step)


def store(half, out, done, core):
    rows = half.shape[0]
    copy = pltpu.make_async_copy(half, out.at[pl.ds(pl.multiple_of(core * rows, rows), rows), :], done)
    copy.start()
    copy.wait()


def store_mine_kernel(half, out, done):
    store(half, out, done, lax.axis_index("core"))


def store_other_kernel(half, _, out, done):
    store(half, out, done, 1 - lax.axis_index("core"))


def store_mine(half):
    rows, length = half.shape
    return pl.pallas_call(
        store_mine_kernel,
        in_specs=[VMEM],
        out_specs=HBM,
        out_shape=jax.ShapeDtypeStruct((2 * rows, length), half.dtype),
        scratch_shapes=[pltpu.SemaphoreType.DMA],
        compiler_params=LIMIT,
        name="store_mine",
    )(half)


def store_other(half, out):
    return pl.pallas_call(
        store_other_kernel,
        in_specs=[VMEM, HBM],
        out_specs=HBM,
        out_shape=jax.ShapeDtypeStruct(out.shape, out.dtype),
        scratch_shapes=[pltpu.SemaphoreType.DMA],
        input_output_aliases={1: 0},
        compiler_params=LIMIT,
        name="store_other",
    )(half, out)


def shards(grads, signs, dither):
    _, rows, length = grads.shape
    chips = lax.axis_size(CHIPS)
    swap = [(0, 1), (1, 0)]
    matrix = signs_matrix(length // 2)
    mean_rows = rows // 2 // chips

    own, own_dither, send, tops, matrix, own_signs = rotate(
        grads[0], signs, dither[0], matrix, mean_rows, lax.axis_size(NEAR)
    )
    received = lax.ppermute(send, "core", swap)

    tops = highest(exchange(tops, NEAR), lax.axis_size(FAR))
    tops = exchange(tops, FAR)

    codes, quant_step = chip_codes(tops, own, own_dither, received)
    codes = lax.all_to_all(codes.reshape(chips, mean_rows, length), CHIPS, 0, 0)

    mean = owned_mean(CORES * chips, codes, own_signs, matrix, quant_step)
    mean = lax.all_to_all(mean, CHIPS, 0, 0).reshape(rows // 2, length)

    other = lax.ppermute(mean, "core", swap)
    mean_grad = store_other(other, store_mine(mean))
    return (mean_grad, quant_step.reshape(()))


def solution(mesh):
    tensor = mesh.shape["tensor"]
    devices = mesh.devices.reshape(-1, Z, CORES, tensor)
    fine = Mesh(devices, ("x", "z", "core", "tensor"))
    dp = ("x", "z", "core")
    return jax.shard_map(
        shards,
        mesh=fine,
        in_specs=(P(dp, "tensor", None), P("tensor", None), P(dp, "tensor", None)),
        out_specs=(P("tensor", None), P()),
        check_vma=False,
    )
```

```python
import math

import jax
import jax.numpy as jnp
import numpy as np
from jax import lax
from jax.experimental import pallas as pl
from jax.experimental.pallas import tpu as pltpu
from jax.sharding import Mesh, PartitionSpec as P

Z, CORES = 8, 2
CHIPS = ("x", "z")
NEAR, FAR = ("core", "tensor"), ("x", "z")
STRIPE = 64


def signs_matrix(length):
    matrix = np.ones((1, 1), np.float32)
    while matrix.shape[0] < length:
        matrix = np.block([[matrix, matrix], [matrix, -matrix]])
    return jnp.asarray(matrix, jnp.bfloat16)


def butterfly(values):
    half = values.shape[1] // 2
    left, right = values[:, :half], values[:, half:]
    return jnp.concatenate([left + right, left - right], axis=0)


def parts_of(values, count):
    parts = []
    for _ in range(count):
        part = values.astype(jnp.bfloat16)
        parts.append(part)
        values = values - part.astype(jnp.float32)
    return parts


def transform(values, matrix, count):
    rows, length = values.shape
    parts = jnp.concatenate(parts_of(butterfly(values), count), axis=0)
    products = jnp.dot(parts, matrix, preferred_element_type=jnp.float32)
    out = products[-2 * rows :]
    for i in range(count - 2, -1, -1):
        out = out + products[2 * rows * i : 2 * rows * (i + 1)]
    out = out * (1.0 / math.sqrt(length))
    return jnp.concatenate([out[:rows], out[rows:]], axis=1)


def rotate_kernel(
    grads, signs, dither, matrix_in, own, own_dither, send, tops, matrix, own_signs,
    grads_buf, signs_buf, dither_buf, fetched, kept,
):
    rows, length = grads.shape
    half = rows // 2
    mine = lax.axis_index("core") * half
    others = half - mine
    low, high = pl.ds(0, half), pl.ds(half, half)

    def at(start):
        return pl.ds(pl.multiple_of(start, half), half)

    def fetch(source, start, target, place, semaphore):
        return pltpu.make_async_copy(source.at[at(start), :], target.at[place, :], semaphore)

    stages = [
        (place, fetch(grads, start, grads_buf, place, fetched.at[0, i]), fetch(signs, start, signs_buf, place, fetched.at[1, i]))
        for i, (place, start) in enumerate(((low, others), (high, mine)))
    ]
    get_matrix = pltpu.make_async_copy(matrix_in, matrix, kept.at[0])
    get_others = pltpu.make_async_copy(dither.at[at(others), :], dither_buf, kept.at[1])
    get_mine = pltpu.make_async_copy(dither.at[at(mine), :], own_dither, kept.at[2])
    get_matrix.start()
    for _, get_grads, get_signs in stages:
        get_grads.start()
        get_signs.start()
    get_others.start()
    get_mine.start()
    get_matrix.wait()

    top = jnp.zeros((8, length), jnp.float32)
    for (place, get_grads, get_signs), result in zip(stages, (send, own)):
        get_grads.wait()
        get_signs.wait()
        rotated = transform(grads_buf[place, :] * signs_buf[place, :].astype(jnp.float32), matrix[...], 3)
        top = jnp.maximum(top, jnp.max(jnp.abs(rotated).reshape(half // 8, 8, length), axis=0))
        result[low, :] = rotated
    tops[...] = jnp.full(tops.shape, jnp.max(top), jnp.float32)
    get_others.wait()
    send[high, :] = dither_buf[...].astype(jnp.float32)
    mean_rows = own_signs.shape[0]
    chip = lax.axis_index("x") * lax.axis_size("z") + lax.axis_index("z")
    here = pl.ds(pl.multiple_of(half + chip * mean_rows, mean_rows), mean_rows)
    own_signs[...] = signs_buf[here, :].astype(jnp.float32)
    get_mine.wait()


VMEM = pl.BlockSpec(memory_space=pltpu.VMEM)
SMEM = pl.BlockSpec(memory_space=pltpu.SMEM)
HBM = pl.BlockSpec(memory_space=pltpu.HBM)
LIMIT = pltpu.CompilerParams(vmem_limit_bytes=16 * 2**20)


def rotate(grads, signs, dither, matrix, mean_rows, peers):
    rows, length = grads.shape
    half = rows // 2
    return pl.pallas_call(
        rotate_kernel,
        in_specs=[HBM] * 4,
        out_specs=[VMEM] * 6,
        out_shape=[
            jax.ShapeDtypeStruct((half, length), jnp.float32),
            jax.ShapeDtypeStruct((half, length), jnp.int32),
            jax.ShapeDtypeStruct((rows, length), jnp.float32),
            jax.ShapeDtypeStruct((peers, 128), jnp.float32),
            jax.ShapeDtypeStruct(matrix.shape, matrix.dtype),
            jax.ShapeDtypeStruct((mean_rows, length), jnp.float32),
        ],
        scratch_shapes=[
            pltpu.VMEM((rows, length), jnp.float32),
            pltpu.VMEM((rows, length), jnp.int32),
            pltpu.VMEM((half, length), jnp.int32),
            pltpu.SemaphoreType.DMA((2, 2)),
            pltpu.SemaphoreType.DMA((3,)),
        ],
        compiler_params=LIMIT,
        name="rotate",
    )(*(pltpu.with_memory_space_constraint(a, pltpu.HBM) for a in (grads, signs, dither, matrix)))


def highest_kernel(tops, out):
    out[...] = jnp.broadcast_to(jnp.max(tops[...], axis=0, keepdims=True), out.shape)


def highest(tops, peers):
    return pl.pallas_call(
        highest_kernel,
        in_specs=[VMEM],
        out_specs=VMEM,
        out_shape=jax.ShapeDtypeStruct((peers, 128), jnp.float32),
        compiler_params=LIMIT,
        name="highest",
    )(tops)


def exchange(tops, axes):
    peers, lanes = tops.shape
    return lax.all_to_all(tops.reshape(peers, 1, lanes), axes, 0, 0).reshape(peers, lanes)


def codes_kernel(tops, own, dither, received, codes):
    half, length = own.shape
    top = jnp.max(tops[...], axis=0, keepdims=True)
    scale = jnp.concatenate([127.0 / top] * (length // 128), axis=1)
    for i in range(0, half, STRIPE):
        here, there = pl.ds(i, STRIPE), pl.ds(half + i, STRIPE)
        first = jnp.floor(own[here, :] * scale + dither[here, :].astype(jnp.float32) * 2.0 ** (-12))
        second = jnp.floor(received[here, :] * scale + received[there, :] * 2.0 ** (-12))
        codes[here, :] = first + second


def chip_codes(tops, own, dither, received):
    return pl.pallas_call(
        codes_kernel,
        in_specs=[VMEM] * 4,
        out_specs=VMEM,
        out_shape=jax.ShapeDtypeStruct(own.shape, jnp.float32),
        compiler_params=LIMIT,
        name="chip_codes",
    )(tops, own, dither, received)


def mean_kernel(replicas, tops, codes, signs, matrix, out):
    total = jnp.sum(codes[...], axis=0)
    back = transform(total, matrix[...], 2)
    factor = jnp.max(tops[...], axis=0, keepdims=True) / 127.0 * (1.0 / replicas)
    factor = jnp.concatenate([factor] * (total.shape[1] // 128), axis=1)
    mean = signs[...] * (back * factor)
    out[...] = jnp.broadcast_to(mean[None], out.shape)


def owned_mean(replicas, tops, codes, signs, matrix):
    return pl.pallas_call(
        lambda *refs: mean_kernel(replicas, *refs),
        in_specs=[VMEM] * 4,
        out_specs=VMEM,
        out_shape=jax.ShapeDtypeStruct(codes.shape, jnp.float32),
        compiler_params=LIMIT,
        name="owned_mean",
    )(tops, codes, signs, matrix)


def store(half, out, done, core):
    rows = half.shape[0]
    copy = pltpu.make_async_copy(half, out.at[pl.ds(pl.multiple_of(core * rows, rows), rows), :], done)
    copy.start()
    copy.wait()


def store_mine_kernel(half, tops, out, quant_step, done):
    quant_step[0, 0] = jnp.max(tops[...] / 127.0)
    store(half, out, done, lax.axis_index("core"))


def store_other_kernel(half, _, out, done):
    store(half, out, done, 1 - lax.axis_index("core"))


def store_mine(half, tops):
    rows, length = half.shape
    return pl.pallas_call(
        store_mine_kernel,
        in_specs=[VMEM, VMEM],
        out_specs=[HBM, SMEM],
        out_shape=[
            jax.ShapeDtypeStruct((2 * rows, length), half.dtype),
            jax.ShapeDtypeStruct((1, 1), jnp.float32),
        ],
        scratch_shapes=[pltpu.SemaphoreType.DMA],
        compiler_params=LIMIT,
        name="store_mine",
    )(half, tops)


def store_other(half, out):
    return pl.pallas_call(
        store_other_kernel,
        in_specs=[VMEM, HBM],
        out_specs=HBM,
        out_shape=jax.ShapeDtypeStruct(out.shape, out.dtype),
        scratch_shapes=[pltpu.SemaphoreType.DMA],
        input_output_aliases={1: 0},
        compiler_params=LIMIT,
        name="store_other",
    )(half, out)


def shards(grads, signs, dither):
    _, rows, length = grads.shape
    chips = lax.axis_size(CHIPS)
    swap = [(0, 1), (1, 0)]
    matrix = signs_matrix(length // 2)
    mean_rows = rows // 2 // chips

    own, own_dither, send, tops, matrix, own_signs = rotate(
        grads[0], signs, dither[0], matrix, mean_rows, lax.axis_size(NEAR)
    )
    received = lax.ppermute(send, "core", swap)

    tops = highest(exchange(tops, NEAR), lax.axis_size(FAR))
    tops = exchange(tops, FAR)

    codes = chip_codes(tops, own, own_dither, received)
    codes = lax.all_to_all(codes.reshape(chips, mean_rows, length), CHIPS, 0, 0)

    mean = owned_mean(CORES * chips, tops, codes, own_signs, matrix)
    mean = lax.all_to_all(mean, CHIPS, 0, 0).reshape(rows // 2, length)

    other = lax.ppermute(mean, "core", swap)
    mean_grad, quant_step = store_mine(mean, tops)
    mean_grad = store_other(other, mean_grad)
    return (mean_grad, quant_step.reshape(()))


def solution(mesh):
    tensor = mesh.shape["tensor"]
    devices = mesh.devices.reshape(-1, Z, CORES, tensor)
    fine = Mesh(devices, ("x", "z", "core", "tensor"))
    dp = ("x", "z", "core")
    return jax.shard_map(
        shards,
        mesh=fine,
        in_specs=(P(dp, "tensor", None), P("tensor", None), P(dp, "tensor", None)),
        out_specs=(P("tensor", None), P()),
        check_vma=False,
    )
```

```python
import math

import jax
import jax.numpy as jnp
import numpy as np
from jax import lax
from jax.experimental import pallas as pl
from jax.experimental.pallas import tpu as pltpu
from jax.sharding import Mesh, PartitionSpec as P

Z, CORES = 8, 2
CHIPS = ("x", "z")
NEAR, FAR = ("core", "tensor"), ("x", "z")
STRIPE = 64


def signs_matrix(length):
    matrix = np.ones((1, 1), np.float32)
    while matrix.shape[0] < length:
        matrix = np.block([[matrix, matrix], [matrix, -matrix]])
    return jnp.asarray(matrix, jnp.bfloat16)


def butterfly(values):
    half = values.shape[1] // 2
    left, right = values[:, :half], values[:, half:]
    return jnp.concatenate([left + right, left - right], axis=0)


def parts_of(values, count):
    parts = []
    for _ in range(count):
        part = values.astype(jnp.bfloat16)
        parts.append(part)
        values = values - part.astype(jnp.float32)
    return parts


def transform(values, matrix, count):
    rows, length = values.shape
    parts = jnp.concatenate(parts_of(butterfly(values), count), axis=0)
    products = jnp.dot(parts, matrix, preferred_element_type=jnp.float32)
    out = products[-2 * rows :]
    for i in range(count - 2, -1, -1):
        out = out + products[2 * rows * i : 2 * rows * (i + 1)]
    out = out * (1.0 / math.sqrt(length))
    return jnp.concatenate([out[:rows], out[rows:]], axis=1)


def rotate_kernel(
    grads, signs, dither, matrix_in, own, own_dither, send, tops, matrix, own_signs,
    grads_buf, signs_buf, dither_buf, fetched, kept,
):
    rows, length = grads.shape
    half = rows // 2
    mine = lax.axis_index("core") * half
    others = half - mine
    low, high = pl.ds(0, half), pl.ds(half, half)

    def at(start):
        return pl.ds(pl.multiple_of(start, half), half)

    def fetch(source, start, target, place, semaphore):
        return pltpu.make_async_copy(source.at[at(start), :], target.at[place, :], semaphore)

    stages = [
        (place, fetch(grads, start, grads_buf, place, fetched.at[0, i]), fetch(signs, start, signs_buf, place, fetched.at[1, i]))
        for i, (place, start) in enumerate(((low, others), (high, mine)))
    ]
    get_matrix = pltpu.make_async_copy(matrix_in, matrix, kept.at[0])
    get_others = pltpu.make_async_copy(dither.at[at(others), :], dither_buf, kept.at[1])
    get_mine = pltpu.make_async_copy(dither.at[at(mine), :], own_dither, kept.at[2])
    get_matrix.start()
    for _, get_grads, get_signs in stages:
        get_grads.start()
        get_signs.start()
    get_others.start()
    get_mine.start()
    get_matrix.wait()

    top = jnp.zeros((8, length), jnp.float32)
    for (place, get_grads, get_signs), result in zip(stages, (send, own)):
        get_grads.wait()
        get_signs.wait()
        rotated = transform(grads_buf[place, :] * signs_buf[place, :].astype(jnp.float32), matrix[...], 3)
        top = jnp.maximum(top, jnp.max(jnp.abs(rotated).reshape(half // 8, 8, length), axis=0))
        result[low, :] = rotated
    tops[...] = jnp.full(tops.shape, jnp.max(top), jnp.float32)
    get_others.wait()
    send[high, :] = dither_buf[...].astype(jnp.float32)
    mean_rows = own_signs.shape[0]
    chip = lax.axis_index("x") * lax.axis_size("z") + lax.axis_index("z")
    here = pl.ds(pl.multiple_of(half + chip * mean_rows, mean_rows), mean_rows)
    own_signs[...] = signs_buf[here, :].astype(jnp.float32)
    get_mine.wait()


VMEM = pl.BlockSpec(memory_space=pltpu.VMEM)
SMEM = pl.BlockSpec(memory_space=pltpu.SMEM)
HBM = pl.BlockSpec(memory_space=pltpu.HBM)
LIMIT = pltpu.CompilerParams(vmem_limit_bytes=16 * 2**20)


def rotate(grads, signs, dither, matrix, mean_rows, peers):
    rows, length = grads.shape
    half = rows // 2
    return pl.pallas_call(
        rotate_kernel,
        in_specs=[HBM] * 4,
        out_specs=[VMEM] * 6,
        out_shape=[
            jax.ShapeDtypeStruct((half, length), jnp.float32),
            jax.ShapeDtypeStruct((half, length), jnp.int32),
            jax.ShapeDtypeStruct((rows, length), jnp.float32),
            jax.ShapeDtypeStruct((peers, 128), jnp.float32),
            jax.ShapeDtypeStruct(matrix.shape, matrix.dtype),
            jax.ShapeDtypeStruct((mean_rows, length), jnp.float32),
        ],
        scratch_shapes=[
            pltpu.VMEM((rows, length), jnp.float32),
            pltpu.VMEM((rows, length), jnp.int32),
            pltpu.VMEM((half, length), jnp.int32),
            pltpu.SemaphoreType.DMA((2, 2)),
            pltpu.SemaphoreType.DMA((3,)),
        ],
        compiler_params=LIMIT,
        name="rotate",
    )(*(pltpu.with_memory_space_constraint(a, pltpu.HBM) for a in (grads, signs, dither, matrix)))


def highest_kernel(tops, out):
    out[...] = jnp.broadcast_to(jnp.max(tops[...], axis=0, keepdims=True), out.shape)


def highest(tops, peers):
    return pl.pallas_call(
        highest_kernel,
        in_specs=[VMEM],
        out_specs=VMEM,
        out_shape=jax.ShapeDtypeStruct((peers, 128), jnp.float32),
        compiler_params=LIMIT,
        cost_estimate=pl.CostEstimate(flops=3 * 10**10, bytes_accessed=0, transcendentals=0),
        name="highest",
    )(tops)


def exchange(tops, axes):
    peers, lanes = tops.shape
    return lax.all_to_all(tops.reshape(peers, 1, lanes), axes, 0, 0).reshape(peers, lanes)


def codes_kernel(tops, own, dither, received, codes):
    half, length = own.shape
    top = jnp.max(tops[...], axis=0, keepdims=True)
    scale = jnp.concatenate([127.0 / top] * (length // 128), axis=1)
    for i in range(0, half, STRIPE):
        here, there = pl.ds(i, STRIPE), pl.ds(half + i, STRIPE)
        first = jnp.floor(own[here, :] * scale + dither[here, :].astype(jnp.float32) * 2.0 ** (-12))
        second = jnp.floor(received[here, :] * scale + received[there, :] * 2.0 ** (-12))
        codes[here, :] = first + second


def chip_codes(tops, own, dither, received):
    return pl.pallas_call(
        codes_kernel,
        in_specs=[VMEM] * 4,
        out_specs=VMEM,
        out_shape=jax.ShapeDtypeStruct(own.shape, jnp.float32),
        compiler_params=LIMIT,
        name="chip_codes",
    )(tops, own, dither, received)


def mean_kernel(replicas, tops, codes, signs, matrix, out):
    total = jnp.sum(codes[...], axis=0)
    back = transform(total, matrix[...], 2)
    factor = jnp.max(tops[...], axis=0, keepdims=True) / 127.0 * (1.0 / replicas)
    factor = jnp.concatenate([factor] * (total.shape[1] // 128), axis=1)
    mean = signs[...] * (back * factor)
    out[...] = jnp.broadcast_to(mean[None], out.shape)


def owned_mean(replicas, tops, codes, signs, matrix):
    return pl.pallas_call(
        lambda *refs: mean_kernel(replicas, *refs),
        in_specs=[VMEM] * 4,
        out_specs=VMEM,
        out_shape=jax.ShapeDtypeStruct(codes.shape, jnp.float32),
        compiler_params=LIMIT,
        name="owned_mean",
    )(tops, codes, signs, matrix)


def store(half, out, done, core):
    rows = half.shape[0]
    copy = pltpu.make_async_copy(half, out.at[pl.ds(pl.multiple_of(core * rows, rows), rows), :], done)
    copy.start()
    copy.wait()


def store_mine_kernel(half, tops, out, quant_step, done):
    quant_step[0, 0] = jnp.max(tops[...] / 127.0)
    store(half, out, done, lax.axis_index("core"))


def store_other_kernel(half, _, out, done):
    store(half, out, done, 1 - lax.axis_index("core"))


def store_mine(half, tops):
    rows, length = half.shape
    return pl.pallas_call(
        store_mine_kernel,
        in_specs=[VMEM, VMEM],
        out_specs=[HBM, SMEM],
        out_shape=[
            jax.ShapeDtypeStruct((2 * rows, length), half.dtype),
            jax.ShapeDtypeStruct((1, 1), jnp.float32),
        ],
        scratch_shapes=[pltpu.SemaphoreType.DMA],
        compiler_params=LIMIT,
        name="store_mine",
    )(half, tops)


def store_other(half, out):
    return pl.pallas_call(
        store_other_kernel,
        in_specs=[VMEM, HBM],
        out_specs=HBM,
        out_shape=jax.ShapeDtypeStruct(out.shape, out.dtype),
        scratch_shapes=[pltpu.SemaphoreType.DMA],
        input_output_aliases={1: 0},
        compiler_params=LIMIT,
        name="store_other",
    )(half, out)


def shards(grads, signs, dither):
    _, rows, length = grads.shape
    chips = lax.axis_size(CHIPS)
    swap = [(0, 1), (1, 0)]
    matrix = signs_matrix(length // 2)
    mean_rows = rows // 2 // chips

    own, own_dither, send, tops, matrix, own_signs = rotate(
        grads[0], signs, dither[0], matrix, mean_rows, lax.axis_size(NEAR)
    )
    tops = exchange(tops, NEAR)
    received = lax.ppermute(send, "core", swap)
    tops = exchange(highest(tops, lax.axis_size(FAR)), FAR)

    codes = chip_codes(tops, own, own_dither, received)
    codes = lax.all_to_all(codes.reshape(chips, mean_rows, length), CHIPS, 0, 0)

    mean = owned_mean(CORES * chips, tops, codes, own_signs, matrix)
    mean = lax.all_to_all(mean, CHIPS, 0, 0).reshape(rows // 2, length)

    other = lax.ppermute(mean, "core", swap)
    mean_grad, quant_step = store_mine(mean, tops)
    mean_grad = store_other(other, mean_grad)
    return (mean_grad, quant_step.reshape(()))


def solution(mesh):
    tensor = mesh.shape["tensor"]
    devices = mesh.devices.reshape(-1, Z, CORES, tensor)
    fine = Mesh(devices, ("x", "z", "core", "tensor"))
    dp = ("x", "z", "core")
    return jax.shard_map(
        shards,
        mesh=fine,
        in_specs=(P(dp, "tensor", None), P("tensor", None), P(dp, "tensor", None)),
        out_specs=(P("tensor", None), P()),
        check_vma=False,
    )
```

```python
import math

import jax
import jax.numpy as jnp
import numpy as np
from jax import lax
from jax.experimental import pallas as pl
from jax.experimental.pallas import tpu as pltpu
from jax.sharding import Mesh, PartitionSpec as P

Z, CORES = 8, 2
CHIPS = ("x", "z")
NEAR, FAR = ("core", "tensor"), ("x", "z")
STRIPE = 64
FIRST = {"x": 2, "z": 5, "tensor": 4}


def signs_matrix(length):
    matrix = np.ones((1, 1), np.float32)
    while matrix.shape[0] < length:
        matrix = np.block([[matrix, matrix], [matrix, -matrix]])
    return jnp.asarray(matrix, jnp.bfloat16)


def butterfly(values):
    half = values.shape[1] // 2
    left, right = values[:, :half], values[:, half:]
    return jnp.concatenate([left + right, left - right], axis=0)


def parts_of(values, count):
    parts = []
    for _ in range(count):
        part = values.astype(jnp.bfloat16)
        parts.append(part)
        values = values - part.astype(jnp.float32)
    return parts


def transform(values, matrix, count):
    rows, length = values.shape
    parts = jnp.concatenate(parts_of(butterfly(values), count), axis=0)
    products = jnp.dot(parts, matrix, preferred_element_type=jnp.float32)
    out = products[-2 * rows :]
    for i in range(count - 2, -1, -1):
        out = out + products[2 * rows * i : 2 * rows * (i + 1)]
    out = out * (1.0 / math.sqrt(length))
    return jnp.concatenate([out[:rows], out[rows:]], axis=1)


def counted(axis):
    size = lax.axis_size(axis)
    return lax.rem(lax.axis_index(axis) + (size - FIRST[axis] % size), size)


def rotate_kernel(
    grads, signs, dither, matrix_in, own, own_dither, send, tops, matrix, own_signs,
    grads_buf, signs_buf, dither_buf, fetched, kept,
):
    rows, length = grads.shape
    half = rows // 2
    mine = lax.axis_index("core") * half
    others = half - mine
    low, high = pl.ds(0, half), pl.ds(half, half)

    def at(start):
        return pl.ds(pl.multiple_of(start, half), half)

    def fetch(source, start, target, place, semaphore):
        return pltpu.make_async_copy(source.at[at(start), :], target.at[place, :], semaphore)

    stages = [
        (place, fetch(grads, start, grads_buf, place, fetched.at[0, i]), fetch(signs, start, signs_buf, place, fetched.at[1, i]))
        for i, (place, start) in enumerate(((low, others), (high, mine)))
    ]
    get_matrix = pltpu.make_async_copy(matrix_in, matrix, kept.at[0])
    get_others = pltpu.make_async_copy(dither.at[at(others), :], dither_buf, kept.at[1])
    get_mine = pltpu.make_async_copy(dither.at[at(mine), :], own_dither, kept.at[2])
    get_matrix.start()
    for _, get_grads, get_signs in stages:
        get_grads.start()
        get_signs.start()
    get_others.start()
    get_mine.start()
    get_matrix.wait()

    top = jnp.zeros((8, length), jnp.float32)
    for (place, get_grads, get_signs), result in zip(stages, (send, own)):
        get_grads.wait()
        get_signs.wait()
        rotated = transform(grads_buf[place, :] * signs_buf[place, :].astype(jnp.float32), matrix[...], 3)
        top = jnp.maximum(top, jnp.max(jnp.abs(rotated).reshape(half // 8, 8, length), axis=0))
        result[low, :] = rotated
    tops[...] = jnp.full(tops.shape, jnp.max(top), jnp.float32)
    get_others.wait()
    send[high, :] = dither_buf[...].astype(jnp.float32)
    mean_rows = own_signs.shape[0]
    chip = counted("x") * lax.axis_size("z") + counted("z")
    here = pl.ds(pl.multiple_of(half + chip * mean_rows, mean_rows), mean_rows)
    own_signs[...] = signs_buf[here, :].astype(jnp.float32)
    get_mine.wait()


VMEM = pl.BlockSpec(memory_space=pltpu.VMEM)
SMEM = pl.BlockSpec(memory_space=pltpu.SMEM)
HBM = pl.BlockSpec(memory_space=pltpu.HBM)
LIMIT = pltpu.CompilerParams(vmem_limit_bytes=16 * 2**20)


def rotate(grads, signs, dither, matrix, mean_rows, peers):
    rows, length = grads.shape
    half = rows // 2
    return pl.pallas_call(
        rotate_kernel,
        in_specs=[HBM] * 4,
        out_specs=[VMEM] * 6,
        out_shape=[
            jax.ShapeDtypeStruct((half, length), jnp.float32),
            jax.ShapeDtypeStruct((half, length), jnp.int32),
            jax.ShapeDtypeStruct((rows, length), jnp.float32),
            jax.ShapeDtypeStruct((peers, 128), jnp.float32),
            jax.ShapeDtypeStruct(matrix.shape, matrix.dtype),
            jax.ShapeDtypeStruct((mean_rows, length), jnp.float32),
        ],
        scratch_shapes=[
            pltpu.VMEM((rows, length), jnp.float32),
            pltpu.VMEM((rows, length), jnp.int32),
            pltpu.VMEM((half, length), jnp.int32),
            pltpu.SemaphoreType.DMA((2, 2)),
            pltpu.SemaphoreType.DMA((3,)),
        ],
        compiler_params=LIMIT,
        name="rotate",
    )(*(pltpu.with_memory_space_constraint(a, pltpu.HBM) for a in (grads, signs, dither, matrix)))


def highest_kernel(tops, out):
    out[...] = jnp.broadcast_to(jnp.max(tops[...], axis=0, keepdims=True), out.shape)


def highest(tops, peers):
    return pl.pallas_call(
        highest_kernel,
        in_specs=[VMEM],
        out_specs=VMEM,
        out_shape=jax.ShapeDtypeStruct((peers, 128), jnp.float32),
        compiler_params=LIMIT,
        cost_estimate=pl.CostEstimate(flops=3 * 10**10, bytes_accessed=0, transcendentals=0),
        name="highest",
    )(tops)


def all_to_all(values, axes):
    sizes = [lax.axis_size(axis) for axis in axes]
    peers = np.arange(math.prod(sizes)).reshape(sizes)
    for dim, axis in enumerate(axes):
        peers = np.roll(peers, -FIRST.get(axis, 0), dim)
    group = [int(peer) for peer in peers.reshape(-1)]
    return lax.all_to_all(values, axes, 0, 0, axis_index_groups=[group])


def exchange(tops, axes):
    peers, lanes = tops.shape
    return all_to_all(tops.reshape(peers, 1, lanes), axes).reshape(peers, lanes)


def codes_kernel(tops, own, dither, received, codes):
    half, length = own.shape
    top = jnp.max(tops[...], axis=0, keepdims=True)
    scale = jnp.concatenate([127.0 / top] * (length // 128), axis=1)
    for i in range(0, half, STRIPE):
        here, there = pl.ds(i, STRIPE), pl.ds(half + i, STRIPE)
        first = jnp.floor(own[here, :] * scale + dither[here, :].astype(jnp.float32) * 2.0 ** (-12))
        second = jnp.floor(received[here, :] * scale + received[there, :] * 2.0 ** (-12))
        codes[here, :] = first + second


def chip_codes(tops, own, dither, received):
    return pl.pallas_call(
        codes_kernel,
        in_specs=[VMEM] * 4,
        out_specs=VMEM,
        out_shape=jax.ShapeDtypeStruct(own.shape, jnp.float32),
        compiler_params=LIMIT,
        name="chip_codes",
    )(tops, own, dither, received)


def mean_kernel(replicas, tops, codes, signs, matrix, out):
    total = jnp.sum(codes[...], axis=0)
    back = transform(total, matrix[...], 2)
    factor = jnp.max(tops[...], axis=0, keepdims=True) / 127.0 * (1.0 / replicas)
    factor = jnp.concatenate([factor] * (total.shape[1] // 128), axis=1)
    mean = signs[...] * (back * factor)
    out[...] = jnp.broadcast_to(mean[None], out.shape)


def owned_mean(replicas, tops, codes, signs, matrix):
    return pl.pallas_call(
        lambda *refs: mean_kernel(replicas, *refs),
        in_specs=[VMEM] * 4,
        out_specs=VMEM,
        out_shape=jax.ShapeDtypeStruct(codes.shape, jnp.float32),
        compiler_params=LIMIT,
        name="owned_mean",
    )(tops, codes, signs, matrix)


def store(half, out, done, core):
    rows = half.shape[0]
    copy = pltpu.make_async_copy(half, out.at[pl.ds(pl.multiple_of(core * rows, rows), rows), :], done)
    copy.start()
    copy.wait()


def store_mine_kernel(half, tops, out, quant_step, done):
    quant_step[0, 0] = jnp.max(tops[...] / 127.0)
    store(half, out, done, lax.axis_index("core"))


def store_other_kernel(half, _, out, done):
    store(half, out, done, 1 - lax.axis_index("core"))


def store_mine(half, tops):
    rows, length = half.shape
    return pl.pallas_call(
        store_mine_kernel,
        in_specs=[VMEM, VMEM],
        out_specs=[HBM, SMEM],
        out_shape=[
            jax.ShapeDtypeStruct((2 * rows, length), half.dtype),
            jax.ShapeDtypeStruct((1, 1), jnp.float32),
        ],
        scratch_shapes=[pltpu.SemaphoreType.DMA],
        compiler_params=LIMIT,
        name="store_mine",
    )(half, tops)


def store_other(half, out):
    return pl.pallas_call(
        store_other_kernel,
        in_specs=[VMEM, HBM],
        out_specs=HBM,
        out_shape=jax.ShapeDtypeStruct(out.shape, out.dtype),
        scratch_shapes=[pltpu.SemaphoreType.DMA],
        input_output_aliases={1: 0},
        compiler_params=LIMIT,
        name="store_other",
    )(half, out)


def shards(grads, signs, dither):
    _, rows, length = grads.shape
    chips = lax.axis_size(CHIPS)
    swap = [(0, 1), (1, 0)]
    matrix = signs_matrix(length // 2)
    mean_rows = rows // 2 // chips

    own, own_dither, send, tops, matrix, own_signs = rotate(
        grads[0], signs, dither[0], matrix, mean_rows, lax.axis_size(NEAR)
    )
    tops = exchange(tops, NEAR)
    received = lax.ppermute(send, "core", swap)
    tops = exchange(highest(tops, lax.axis_size(FAR)), FAR)

    codes = chip_codes(tops, own, own_dither, received)
    codes = all_to_all(codes.reshape(chips, mean_rows, length), CHIPS)

    mean = owned_mean(CORES * chips, tops, codes, own_signs, matrix)
    mean = all_to_all(mean, CHIPS).reshape(rows // 2, length)

    other = lax.ppermute(mean, "core", swap)
    mean_grad, quant_step = store_mine(mean, tops)
    mean_grad = store_other(other, mean_grad)
    return (mean_grad, quant_step.reshape(()))


def solution(mesh):
    tensor = mesh.shape["tensor"]
    devices = mesh.devices.reshape(-1, Z, CORES, tensor)
    fine = Mesh(devices, ("x", "z", "core", "tensor"))
    dp = ("x", "z", "core")
    return jax.shard_map(
        shards,
        mesh=fine,
        in_specs=(P(dp, "tensor", None), P("tensor", None), P(dp, "tensor", None)),
        out_specs=(P("tensor", None), P()),
        check_vma=False,
    )
```

```python
import math

import jax
import jax.numpy as jnp
import numpy as np
from jax import lax
from jax.experimental import pallas as pl
from jax.experimental.pallas import tpu as pltpu
from jax.sharding import Mesh, PartitionSpec as P

Z, CORES = 8, 2
CHIPS = ("x", "z")
NEAR, FAR = ("core", "z"), ("x", "tensor")
STRIPE = 64
FIRST = {"x": 2, "z": 5, "tensor": 4}


def signs_matrix(length):
    matrix = np.ones((1, 1), np.float32)
    while matrix.shape[0] < length:
        matrix = np.block([[matrix, matrix], [matrix, -matrix]])
    return jnp.asarray(matrix, jnp.bfloat16)


def butterfly(values):
    half = values.shape[1] // 2
    left, right = values[:, :half], values[:, half:]
    return jnp.concatenate([left + right, left - right], axis=0)


def parts_of(values, count):
    parts = []
    for _ in range(count):
        part = values.astype(jnp.bfloat16)
        parts.append(part)
        values = values - part.astype(jnp.float32)
    return parts


def transform(values, matrix, count):
    rows, length = values.shape
    parts = jnp.concatenate(parts_of(butterfly(values), count), axis=0)
    products = jnp.dot(parts, matrix, preferred_element_type=jnp.float32)
    out = products[-2 * rows :]
    for i in range(count - 2, -1, -1):
        out = out + products[2 * rows * i : 2 * rows * (i + 1)]
    out = out * (1.0 / math.sqrt(length))
    return jnp.concatenate([out[:rows], out[rows:]], axis=1)


def counted(axis):
    size = lax.axis_size(axis)
    return lax.rem(lax.axis_index(axis) + (size - FIRST[axis] % size), size)


def rotate_kernel(
    grads, signs, dither, matrix_in, own, own_dither, send, tops, matrix, own_signs,
    grads_buf, signs_buf, dither_buf, fetched, kept,
):
    rows, length = grads.shape
    half = rows // 2
    mine = lax.axis_index("core") * half
    others = half - mine
    low, high = pl.ds(0, half), pl.ds(half, half)

    def at(start):
        return pl.ds(pl.multiple_of(start, half), half)

    def fetch(source, start, target, place, semaphore):
        return pltpu.make_async_copy(source.at[at(start), :], target.at[place, :], semaphore)

    stages = [
        (place, fetch(grads, start, grads_buf, place, fetched.at[0, i]), fetch(signs, start, signs_buf, place, fetched.at[1, i]))
        for i, (place, start) in enumerate(((low, others), (high, mine)))
    ]
    get_matrix = pltpu.make_async_copy(matrix_in, matrix, kept.at[0])
    get_others = pltpu.make_async_copy(dither.at[at(others), :], dither_buf, kept.at[1])
    get_mine = pltpu.make_async_copy(dither.at[at(mine), :], own_dither, kept.at[2])
    get_matrix.start()
    for _, get_grads, get_signs in stages:
        get_grads.start()
        get_signs.start()
    get_others.start()
    get_mine.start()
    get_matrix.wait()

    top = jnp.zeros((8, length), jnp.float32)
    for (place, get_grads, get_signs), result in zip(stages, (send, own)):
        get_grads.wait()
        get_signs.wait()
        rotated = transform(grads_buf[place, :] * signs_buf[place, :].astype(jnp.float32), matrix[...], 3)
        top = jnp.maximum(top, jnp.max(jnp.abs(rotated).reshape(half // 8, 8, length), axis=0))
        result[low, :] = rotated
    tops[...] = jnp.full(tops.shape, jnp.max(top), jnp.float32)
    get_others.wait()
    send[high, :] = dither_buf[...].astype(jnp.float32)
    mean_rows = own_signs.shape[0]
    chip = counted("x") * lax.axis_size("z") + counted("z")
    here = pl.ds(pl.multiple_of(half + chip * mean_rows, mean_rows), mean_rows)
    own_signs[...] = signs_buf[here, :].astype(jnp.float32)
    get_mine.wait()


VMEM = pl.BlockSpec(memory_space=pltpu.VMEM)
SMEM = pl.BlockSpec(memory_space=pltpu.SMEM)
HBM = pl.BlockSpec(memory_space=pltpu.HBM)
LIMIT = pltpu.CompilerParams(vmem_limit_bytes=16 * 2**20)


def rotate(grads, signs, dither, matrix, mean_rows, peers):
    rows, length = grads.shape
    half = rows // 2
    return pl.pallas_call(
        rotate_kernel,
        in_specs=[HBM] * 4,
        out_specs=[VMEM] * 6,
        out_shape=[
            jax.ShapeDtypeStruct((half, length), jnp.float32),
            jax.ShapeDtypeStruct((half, length), jnp.int32),
            jax.ShapeDtypeStruct((rows, length), jnp.float32),
            jax.ShapeDtypeStruct((peers, 128), jnp.float32),
            jax.ShapeDtypeStruct(matrix.shape, matrix.dtype),
            jax.ShapeDtypeStruct((mean_rows, length), jnp.float32),
        ],
        scratch_shapes=[
            pltpu.VMEM((rows, length), jnp.float32),
            pltpu.VMEM((rows, length), jnp.int32),
            pltpu.VMEM((half, length), jnp.int32),
            pltpu.SemaphoreType.DMA((2, 2)),
            pltpu.SemaphoreType.DMA((3,)),
        ],
        compiler_params=LIMIT,
        name="rotate",
    )(*(pltpu.with_memory_space_constraint(a, pltpu.HBM) for a in (grads, signs, dither, matrix)))


def highest_kernel(tops, out):
    out[...] = jnp.broadcast_to(jnp.max(tops[...], axis=0, keepdims=True), out.shape)


def highest(tops, peers):
    return pl.pallas_call(
        highest_kernel,
        in_specs=[VMEM],
        out_specs=VMEM,
        out_shape=jax.ShapeDtypeStruct((peers, 128), jnp.float32),
        compiler_params=LIMIT,
        cost_estimate=pl.CostEstimate(flops=3 * 10**10, bytes_accessed=0, transcendentals=0),
        name="highest",
    )(tops)


def all_to_all(values, axes):
    sizes = [lax.axis_size(axis) for axis in axes]
    peers = np.arange(math.prod(sizes)).reshape(sizes)
    for dim, axis in enumerate(axes):
        peers = np.roll(peers, -FIRST.get(axis, 0), dim)
    group = [int(peer) for peer in peers.reshape(-1)]
    return lax.all_to_all(values, axes, 0, 0, axis_index_groups=[group])


def exchange(tops, axes):
    peers, lanes = tops.shape
    return all_to_all(tops.reshape(peers, 1, lanes), axes).reshape(peers, lanes)


def codes_kernel(tops, own, dither, received, codes):
    half, length = own.shape
    top = jnp.max(tops[...], axis=0, keepdims=True)
    scale = jnp.concatenate([127.0 / top] * (length // 128), axis=1)
    for i in range(0, half, STRIPE):
        here, there = pl.ds(i, STRIPE), pl.ds(half + i, STRIPE)
        first = jnp.floor(own[here, :] * scale + dither[here, :].astype(jnp.float32) * 2.0 ** (-12))
        second = jnp.floor(received[here, :] * scale + received[there, :] * 2.0 ** (-12))
        codes[here, :] = first + second


def chip_codes(tops, own, dither, received):
    return pl.pallas_call(
        codes_kernel,
        in_specs=[VMEM] * 4,
        out_specs=VMEM,
        out_shape=jax.ShapeDtypeStruct(own.shape, jnp.float32),
        compiler_params=LIMIT,
        name="chip_codes",
    )(tops, own, dither, received)


def mean_kernel(replicas, tops, codes, signs, matrix, out):
    total = jnp.sum(codes[...], axis=0)
    back = transform(total, matrix[...], 2)
    factor = jnp.max(tops[...], axis=0, keepdims=True) / 127.0 * (1.0 / replicas)
    factor = jnp.concatenate([factor] * (total.shape[1] // 128), axis=1)
    mean = signs[...] * (back * factor)
    out[...] = jnp.broadcast_to(mean[None], out.shape)


def owned_mean(replicas, tops, codes, signs, matrix):
    return pl.pallas_call(
        lambda *refs: mean_kernel(replicas, *refs),
        in_specs=[VMEM] * 4,
        out_specs=VMEM,
        out_shape=jax.ShapeDtypeStruct(codes.shape, jnp.float32),
        compiler_params=LIMIT,
        name="owned_mean",
    )(tops, codes, signs, matrix)


def store(half, out, done, core):
    rows = half.shape[0]
    copy = pltpu.make_async_copy(half, out.at[pl.ds(pl.multiple_of(core * rows, rows), rows), :], done)
    copy.start()
    copy.wait()


def store_mine_kernel(half, tops, out, quant_step, done):
    quant_step[0, 0] = jnp.max(tops[...] / 127.0)
    store(half, out, done, lax.axis_index("core"))


def store_other_kernel(half, _, out, done):
    store(half, out, done, 1 - lax.axis_index("core"))


def store_mine(half, tops):
    rows, length = half.shape
    return pl.pallas_call(
        store_mine_kernel,
        in_specs=[VMEM, VMEM],
        out_specs=[HBM, SMEM],
        out_shape=[
            jax.ShapeDtypeStruct((2 * rows, length), half.dtype),
            jax.ShapeDtypeStruct((1, 1), jnp.float32),
        ],
        scratch_shapes=[pltpu.SemaphoreType.DMA],
        compiler_params=LIMIT,
        name="store_mine",
    )(half, tops)


def store_other(half, out):
    return pl.pallas_call(
        store_other_kernel,
        in_specs=[VMEM, HBM],
        out_specs=HBM,
        out_shape=jax.ShapeDtypeStruct(out.shape, out.dtype),
        scratch_shapes=[pltpu.SemaphoreType.DMA],
        input_output_aliases={1: 0},
        compiler_params=LIMIT,
        name="store_other",
    )(half, out)


def shards(grads, signs, dither):
    _, rows, length = grads.shape
    chips = lax.axis_size(CHIPS)
    swap = [(0, 1), (1, 0)]
    matrix = signs_matrix(length // 2)
    mean_rows = rows // 2 // chips

    own, own_dither, send, tops, matrix, own_signs = rotate(
        grads[0], signs, dither[0], matrix, mean_rows, lax.axis_size(NEAR)
    )
    tops = exchange(tops, NEAR)
    received = lax.ppermute(send, "core", swap)
    tops = exchange(highest(tops, lax.axis_size(FAR)), FAR)

    codes = chip_codes(tops, own, own_dither, received)
    codes = all_to_all(codes.reshape(chips, mean_rows, length), CHIPS)

    mean = owned_mean(CORES * chips, tops, codes, own_signs, matrix)
    mean = all_to_all(mean, CHIPS).reshape(rows // 2, length)

    other = lax.ppermute(mean, "core", swap)
    mean_grad, quant_step = store_mine(mean, tops)
    mean_grad = store_other(other, mean_grad)
    return (mean_grad, quant_step.reshape(()))


def solution(mesh):
    tensor = mesh.shape["tensor"]
    devices = mesh.devices.reshape(-1, Z, CORES, tensor)
    fine = Mesh(devices, ("x", "z", "core", "tensor"))
    dp = ("x", "z", "core")
    return jax.shard_map(
        shards,
        mesh=fine,
        in_specs=(P(dp, "tensor", None), P("tensor", None), P(dp, "tensor", None)),
        out_specs=(P("tensor", None), P()),
        check_vma=False,
    )
```

```python
import math

import jax
import jax.numpy as jnp
import numpy as np
from jax import lax
from jax.experimental import pallas as pl
from jax.experimental.pallas import tpu as pltpu
from jax.sharding import Mesh, PartitionSpec as P

Z, CORES = 8, 2
CHIPS = ("x", "z")
NEAR, FAR = ("core", "z"), ("x", "tensor")
STRIPE = 64
FIRST = {"x": 2, "z": 5, "tensor": 4}


def signs_matrix(length):
    matrix = np.ones((1, 1), np.float32)
    while matrix.shape[0] < length:
        matrix = np.block([[matrix, matrix], [matrix, -matrix]])
    return jnp.asarray(matrix, jnp.bfloat16)


def butterfly(values):
    half = values.shape[1] // 2
    left, right = values[:, :half], values[:, half:]
    return jnp.concatenate([left + right, left - right], axis=0)


def parts_of(values, count):
    parts = []
    for _ in range(count):
        part = values.astype(jnp.bfloat16)
        parts.append(part)
        values = values - part.astype(jnp.float32)
    return parts


def transform(values, matrix, count):
    rows, length = values.shape
    parts = jnp.concatenate(parts_of(butterfly(values), count), axis=0)
    products = jnp.dot(parts, matrix, preferred_element_type=jnp.float32)
    out = products[-2 * rows :]
    for i in range(count - 2, -1, -1):
        out = out + products[2 * rows * i : 2 * rows * (i + 1)]
    out = out * (1.0 / math.sqrt(length))
    return jnp.concatenate([out[:rows], out[rows:]], axis=1)


def counted(axis):
    size = lax.axis_size(axis)
    return lax.rem(lax.axis_index(axis) + (size - FIRST[axis] % size), size)


def rotate_kernel(
    grads, signs, dither, matrix_in, own, own_dither, send, tops, matrix, own_signs,
    grads_buf, signs_buf, dither_buf, tops_buf, fetched, kept,
):
    rows, length = grads.shape
    half = rows // 2
    mine = lax.axis_index("core") * half
    others = half - mine
    low, high = pl.ds(0, half), pl.ds(half, half)

    def at(start):
        return pl.ds(pl.multiple_of(start, half), half)

    def fetch(source, start, target, place, semaphore):
        return pltpu.make_async_copy(source.at[at(start), :], target.at[place, :], semaphore)

    stages = [
        (place, fetch(grads, start, grads_buf, place, fetched.at[0, i]), fetch(signs, start, signs_buf, place, fetched.at[1, i]))
        for i, (place, start) in enumerate(((low, others), (high, mine)))
    ]
    get_matrix = pltpu.make_async_copy(matrix_in, matrix, kept.at[0])
    get_others = pltpu.make_async_copy(dither.at[at(others), :], dither_buf, kept.at[1])
    get_mine = pltpu.make_async_copy(dither.at[at(mine), :], own_dither, kept.at[2])
    get_matrix.start()
    for _, get_grads, get_signs in stages:
        get_grads.start()
        get_signs.start()
    get_others.start()
    get_mine.start()
    get_matrix.wait()

    top = jnp.zeros((8, length), jnp.float32)
    for (place, get_grads, get_signs), result in zip(stages, (send, own)):
        get_grads.wait()
        get_signs.wait()
        rotated = transform(grads_buf[place, :] * signs_buf[place, :].astype(jnp.float32), matrix[...], 3)
        top = jnp.maximum(top, jnp.max(jnp.abs(rotated).reshape(half // 8, 8, length), axis=0))
        result[low, :] = rotated
    tops_buf[...] = jnp.full(tops.shape, jnp.max(top), jnp.float32)
    put_tops = pltpu.make_async_copy(tops_buf, tops, kept.at[3])
    put_tops.start()
    get_others.wait()
    send[high, :] = dither_buf[...].astype(jnp.float32)
    mean_rows = own_signs.shape[0]
    chip = counted("x") * lax.axis_size("z") + counted("z")
    here = pl.ds(pl.multiple_of(half + chip * mean_rows, mean_rows), mean_rows)
    own_signs[...] = signs_buf[here, :].astype(jnp.float32)
    get_mine.wait()
    put_tops.wait()


VMEM = pl.BlockSpec(memory_space=pltpu.VMEM)
SMEM = pl.BlockSpec(memory_space=pltpu.SMEM)
HBM = pl.BlockSpec(memory_space=pltpu.HBM)
LIMIT = pltpu.CompilerParams(vmem_limit_bytes=16 * 2**20)


def rotate(grads, signs, dither, matrix, mean_rows, peers):
    rows, length = grads.shape
    half = rows // 2
    return pl.pallas_call(
        rotate_kernel,
        in_specs=[HBM] * 4,
        out_specs=[VMEM, VMEM, VMEM, HBM, VMEM, VMEM],
        out_shape=[
            jax.ShapeDtypeStruct((half, length), jnp.float32),
            jax.ShapeDtypeStruct((half, length), jnp.int32),
            jax.ShapeDtypeStruct((rows, length), jnp.float32),
            jax.ShapeDtypeStruct((peers, 128), jnp.float32),
            jax.ShapeDtypeStruct(matrix.shape, matrix.dtype),
            jax.ShapeDtypeStruct((mean_rows, length), jnp.float32),
        ],
        scratch_shapes=[
            pltpu.VMEM((rows, length), jnp.float32),
            pltpu.VMEM((rows, length), jnp.int32),
            pltpu.VMEM((half, length), jnp.int32),
            pltpu.VMEM((peers, 128), jnp.float32),
            pltpu.SemaphoreType.DMA((2, 2)),
            pltpu.SemaphoreType.DMA((4,)),
        ],
        compiler_params=LIMIT,
        name="rotate",
    )(*(pltpu.with_memory_space_constraint(a, pltpu.HBM) for a in (grads, signs, dither, matrix)))


def highest_kernel(tops, out):
    out[...] = jnp.broadcast_to(jnp.max(tops[...], axis=0, keepdims=True), out.shape)


def highest(tops, peers):
    return pl.pallas_call(
        highest_kernel,
        in_specs=[VMEM],
        out_specs=VMEM,
        out_shape=jax.ShapeDtypeStruct((peers, 128), jnp.float32),
        compiler_params=LIMIT,
        cost_estimate=pl.CostEstimate(flops=3 * 10**10, bytes_accessed=0, transcendentals=0),
        name="highest",
    )(tops)


def all_to_all(values, axes):
    sizes = [lax.axis_size(axis) for axis in axes]
    peers = np.arange(math.prod(sizes)).reshape(sizes)
    for dim, axis in enumerate(axes):
        peers = np.roll(peers, -FIRST.get(axis, 0), dim)
    group = [int(peer) for peer in peers.reshape(-1)]
    return lax.all_to_all(values, axes, 0, 0, axis_index_groups=[group])


def exchange(tops, axes):
    peers, lanes = tops.shape
    return all_to_all(tops.reshape(peers, 1, lanes), axes).reshape(peers, lanes)


def codes_kernel(tops, own, dither, received, codes):
    half, length = own.shape
    top = jnp.max(tops[...], axis=0, keepdims=True)
    scale = jnp.concatenate([127.0 / top] * (length // 128), axis=1)
    for i in range(0, half, STRIPE):
        here, there = pl.ds(i, STRIPE), pl.ds(half + i, STRIPE)
        first = jnp.floor(own[here, :] * scale + dither[here, :].astype(jnp.float32) * 2.0 ** (-12))
        second = jnp.floor(received[here, :] * scale + received[there, :] * 2.0 ** (-12))
        codes[here, :] = first + second


def chip_codes(tops, own, dither, received):
    return pl.pallas_call(
        codes_kernel,
        in_specs=[VMEM] * 4,
        out_specs=VMEM,
        out_shape=jax.ShapeDtypeStruct(own.shape, jnp.float32),
        compiler_params=LIMIT,
        name="chip_codes",
    )(tops, own, dither, received)


def mean_kernel(replicas, tops, codes, signs, matrix, out):
    total = jnp.sum(codes[...], axis=0)
    back = transform(total, matrix[...], 2)
    factor = jnp.max(tops[...], axis=0, keepdims=True) / 127.0 * (1.0 / replicas)
    factor = jnp.concatenate([factor] * (total.shape[1] // 128), axis=1)
    mean = signs[...] * (back * factor)
    out[...] = jnp.broadcast_to(mean[None], out.shape)


def owned_mean(replicas, tops, codes, signs, matrix):
    return pl.pallas_call(
        lambda *refs: mean_kernel(replicas, *refs),
        in_specs=[VMEM] * 4,
        out_specs=VMEM,
        out_shape=jax.ShapeDtypeStruct(codes.shape, jnp.float32),
        compiler_params=LIMIT,
        name="owned_mean",
    )(tops, codes, signs, matrix)


def store(half, out, done, core):
    rows = half.shape[0]
    copy = pltpu.make_async_copy(half, out.at[pl.ds(pl.multiple_of(core * rows, rows), rows), :], done)
    copy.start()
    copy.wait()


def store_mine_kernel(half, tops, out, quant_step, done):
    quant_step[0, 0] = jnp.max(tops[...] / 127.0)
    store(half, out, done, lax.axis_index("core"))


def store_other_kernel(half, _, out, done):
    store(half, out, done, 1 - lax.axis_index("core"))


def store_mine(half, tops):
    rows, length = half.shape
    return pl.pallas_call(
        store_mine_kernel,
        in_specs=[VMEM, VMEM],
        out_specs=[HBM, SMEM],
        out_shape=[
            jax.ShapeDtypeStruct((2 * rows, length), half.dtype),
            jax.ShapeDtypeStruct((1, 1), jnp.float32),
        ],
        scratch_shapes=[pltpu.SemaphoreType.DMA],
        compiler_params=LIMIT,
        name="store_mine",
    )(half, tops)


def store_other(half, out):
    return pl.pallas_call(
        store_other_kernel,
        in_specs=[VMEM, HBM],
        out_specs=HBM,
        out_shape=jax.ShapeDtypeStruct(out.shape, out.dtype),
        scratch_shapes=[pltpu.SemaphoreType.DMA],
        input_output_aliases={1: 0},
        compiler_params=LIMIT,
        name="store_other",
    )(half, out)


def shards(grads, signs, dither):
    _, rows, length = grads.shape
    chips = lax.axis_size(CHIPS)
    swap = [(0, 1), (1, 0)]
    matrix = signs_matrix(length // 2)
    mean_rows = rows // 2 // chips

    own, own_dither, send, tops, matrix, own_signs = rotate(
        grads[0], signs, dither[0], matrix, mean_rows, lax.axis_size(NEAR)
    )
    tops = exchange(tops, NEAR)
    received = lax.ppermute(send, "core", swap)
    tops = exchange(highest(tops, lax.axis_size(FAR)), FAR)

    codes = chip_codes(tops, own, own_dither, received)
    codes = all_to_all(codes.reshape(chips, mean_rows, length), CHIPS)

    mean = owned_mean(CORES * chips, tops, codes, own_signs, matrix)
    mean = all_to_all(mean, CHIPS).reshape(rows // 2, length)

    other = lax.ppermute(mean, "core", swap)
    mean_grad, quant_step = store_mine(mean, tops)
    mean_grad = store_other(other, mean_grad)
    return (mean_grad, quant_step.reshape(()))


def solution(mesh):
    tensor = mesh.shape["tensor"]
    devices = mesh.devices.reshape(-1, Z, CORES, tensor)
    fine = Mesh(devices, ("x", "z", "core", "tensor"))
    dp = ("x", "z", "core")
    return jax.shard_map(
        shards,
        mesh=fine,
        in_specs=(P(dp, "tensor", None), P("tensor", None), P(dp, "tensor", None)),
        out_specs=(P("tensor", None), P()),
        check_vma=False,
    )
```
